512 devices in a mesh: rows: 128 (over z, y, core), grp: 4 (over x).
Axes of the slice: x: 4, y: 4, z: 16, core: 2. Of those that a mesh axis runs over, the one named last changes fastest.
Arguments:
- slab: bfloat16 [294912, 4096], P(('rows', 'grp')), may hold values from -24 to 24
- sketch: bfloat16 [4096, 128], replicated, may hold values from -0.09375 to 0.09375
Outputs:
- basis: float32 [294912, 128], P(('rows', 'grp'))
- projected: bfloat16 [4096, 128], P(('rows', 'grp'))
The draws below stay inside these ranges and needn't reach their ends.
All inputs are finite; a program needn't handle non-finite values.
Results may differ from the reference program's by a relative error of at most 0.0035.
Values sent between devices are 32-bit elements; how exact they have to be, the bound alone decides.
A program may use at most 64 MiB of HBM per device.

```python
import jax
import jax.numpy as jnp

D = 4096
RANK = 128
ROWS = 294912


def with_spikes(entries, key, source, target, shards_of, factor):
    owner, partner = [(jnp.arange(entries.shape[axis_at]) // (entries.shape[axis_at] // shards_of)).reshape([-1 if axis == axis_at else 1 for axis in range(entries.ndim)]) for axis_at in (source, target)]
    chosen = jax.random.permutation(key, shards_of)[partner]
    strong = (owner == chosen) | (owner == (partner + shards_of // 2) % shards_of)
    return jnp.where(strong, factor * entries, entries)


def steps_of(own_key, shape, pieces, low, high):
    level, own = 1.0, jax.random.fold_in(own_key, 6)
    for dim, shards_of in pieces:
        steps = jnp.exp(jax.random.uniform(jax.random.fold_in(own, dim), (shards_of,), jnp.float32, low / len(pieces), high / len(pieces)))
        level = level * jnp.repeat(steps, shape[dim] // shards_of).reshape([-1 if axis == dim else 1 for axis in range(len(shape))])
    return level


def bell_draw(stream_key, dims, scale, bound, shards=(), dtype=jnp.bfloat16):
    entries = jax.random.normal(stream_key, dims, jnp.float32) * scale
    if len(shards) > 0:
        entries = steps_of(stream_key, dims, shards, -0.22, 0.18) * entries
    return jnp.clip(entries, min=-bound, max=bound).astype(dtype)


def noise_with(own_key, dims, spread, most, shards, heavy, kind=jnp.bfloat16):
    result = spread * jax.random.normal(own_key, dims, jnp.float32)
    if shards:
        result = result * steps_of(own_key, dims, shards, -0.22, 0.18)
    return jnp.clip(with_spikes(result, jax.random.fold_in(own_key, 3), *heavy), -most, most).astype(kind)


def setup_inputs(seed: int = 0) -> dict:
    arg_keys = jax.random.split(jax.random.key(seed), 3)
    return {
        "slab": noise_with(arg_keys[0], (ROWS, D), 1.0, 24.0, ((0, 512),), (0, 1, 512, 6.0)),
        "sketch": bell_draw(arg_keys[1], (D, RANK), D ** -0.5, 0.09375),
    }


def orth(matrix):
    factor_q, factor_r = jnp.linalg.qr(matrix)
    signs = jnp.sign(jnp.diagonal(factor_r))
    return factor_q * signs[None, :]

def reference(slab, sketch):
    first = jnp.dot(slab.astype(jnp.float32), sketch.astype(jnp.float32), preferred_element_type=jnp.float32)
    basis_one = orth(first)
    low_one = basis_one.astype(jnp.bfloat16)
    final = jnp.dot(slab.T.astype(jnp.float32), low_one.astype(jnp.float32), preferred_element_type=jnp.float32)
    basis = basis_one * jnp.sqrt(jnp.float32(ROWS))
    projected = (final * jnp.sqrt(jnp.float32(D) / jnp.float32(ROWS))).astype(jnp.bfloat16)
    return (basis, projected)
```

```python
import jax
import jax.numpy as jnp
from jax import lax
from jax.experimental import pallas as pl
from jax.experimental.pallas import tpu as pltpu
from jax.sharding import PartitionSpec as P

MESH = pl.DeviceIdType.MESH
F32, BF16 = jnp.float32, jnp.bfloat16
NZ, NY, NX = 16, 4, 4
LOADS = 4


def place(z, y, c, x):
    return {"rows": (z * NY + y) * 2 + c, "grp": x}


def wait_bytes(ref, sem):
    pltpu.make_async_copy(ref, ref, sem).wait()


def exchange(
    slab, sketch, first, gram, final,
    slab_v, sketch_v, first_t, part, got0, got1, sum1, got2, sum2, got3,
    gram0, gotg1, gotg2,
    load_sem, send_sem, recv0, recv1, recv2, recv3, recvg,
):
    rows_at, x = lax.axis_index("rows"), lax.axis_index("grp")
    z, y, c = rows_at // (2 * NY), (rows_at // 2) % NY, rows_at % 2
    rows = slab.shape[0]
    step = rows // LOADS

    barrier = pltpu.get_barrier_semaphore()
    peers = [
        (z, (y + dy) % NY, (c + dc) % 2, (x + dx) % NX)
        for dy in range(NY) for dx in range(NX) for dc in range(2) if (dy, dx, dc) != (0, 0, 0)
    ] + [((z + d) % NZ, y, c, x) for d in range(1, NZ)]
    for peer in peers:
        pl.semaphore_signal(barrier, inc=1, device_id=place(*peer), device_id_type=MESH)

    sketch_copy = pltpu.make_async_copy(sketch, sketch_v, load_sem.at[LOADS])
    sketch_copy.start()
    loads = [
        pltpu.make_async_copy(slab.at[pl.ds(i * step, step)], slab_v.at[pl.ds(i * step, step)], load_sem.at[i])
        for i in range(LOADS)
    ]
    for load in loads:
        load.start()
    sketch_copy.wait()
    for i, load in enumerate(loads):
        load.wait()
        first[pl.ds(i * step, step), :] = jnp.dot(
            slab_v[pl.ds(i * step, step), :], sketch_v[...], preferred_element_type=F32
        )

    whole = first[...]
    whole_t = whole.T
    local = jnp.dot(whole_t, whole, precision=lax.Precision.HIGHEST, preferred_element_type=F32)
    for q in range(16):
        gram0[q] = local[8 * q : 8 * q + 8, :]
    high = whole_t.astype(BF16)
    low = (whole_t - high.astype(F32)).astype(BF16)
    first_t[...] = jnp.concatenate([high, low], 0)

    pl.semaphore_wait(barrier, len(peers))

    def send(src, dst, at, recv, peer):
        copy = pltpu.make_async_remote_copy(
            src_ref=src, dst_ref=dst, send_sem=send_sem.at[at], recv_sem=recv,
            device_id=place(*peer), device_id_type=MESH,
        )
        copy.start()

    own = y * NX + x
    for dy in range(NY):
        for dx in range(NX):
            ty, tx = (y + dy) % NY, (x + dx) % NX
            slot = (dy * NX + dx) * 2
            if (dy, dx) != (0, 0):
                send(gram0.at[ty * NX + tx], gotg1.at[slot + c], 0, recvg.at[0], (z, ty, 0, tx))

    @pl.when(c == 1)
    def _():
        send(gram0.at[own], gotg1.at[1], 0, recvg.at[0], (z, y, 0, x))

    @pl.when(c == 0)
    def _():
        gotg1[0] = gram0[own]

    wide = 512
    for j in range(8):
        both = jnp.dot(first_t[...], slab_v[:, j * wide : (j + 1) * wide], preferred_element_type=F32)
        sums = both[:128] + both[128:]
        for k in range(4):
            block = sums[:, k * 128 : (k + 1) * 128].T
            at_z, half = (2 * j + k // 2), j // 4
            for yl in range(2):
                for cc in range(2):
                    for xx in range(4):
                        row = ((yl * 2 + cc) * 4 + xx) * 8
                        yy = 2 * (k % 2) + yl
                        a, b = (xx, yy) if half == 0 else (yy, xx)
                        part[cc, half, a, b, at_z % 8] = block[row : row + 8, :]
        if j % 4 == 3:
            half = j // 4
            send(part.at[1 - c, half], got0.at[half], 1 + half, recv0.at[half], (z, y, 1 - c, x))

    @pl.when(c == 0)
    def _():
        wait_bytes(gotg1.at[pl.ds(0, 31)], recvg.at[0])
        tile = gotg1[0]
        for s in range(1, 32):
            tile = tile + gotg1[s]
        gotg2[z] = tile
        for d in range(1, NZ):
            send(gotg2.at[z], gotg2.at[z], 3, recvg.at[1], ((z + d) % NZ, y, c, x))

    def peer_of(half, phase, d):
        if (half + phase) % 2 == 0:
            return (z, y, c, (x + d) % NX)
        return (z, (y + d) % NY, c, x)

    def index_of(half, phase, d):
        return (x + d) % NX if (half + phase) % 2 == 0 else (y + d) % NY

    for half in range(2):
        wait_bytes(got0.at[half], recv0.at[half])
        for d in (2, 1, 3, 0):
            a = index_of(half, 0, d)
            part[c, half, a] = part[c, half, a] + got0[half, a]
            if d:
                send(part.at[c, half, a], got1.at[half, d - 1], 4 + half, recv1.at[half], peer_of(half, 0, d))

    for half in range(2):
        wait_bytes(got1.at[half], recv1.at[half])
        a = index_of(half, 0, 0)
        for d in (2, 1, 3, 0):
            b = index_of(half, 1, d)
            sum1[half, b] = (part[c, half, a, b] + got1[half, 0, b]) + (got1[half, 1, b] + got1[half, 2, b])
            if d:
                send(sum1.at[half, b], got2.at[half, d - 1], 6 + half, recv2.at[half], peer_of(half, 1, d))

    for half in range(2):
        wait_bytes(got2.at[half], recv2.at[half])
        b = index_of(half, 1, 0)
        sum2[pl.ds(8 * half, 8)] = (sum1[half, b] + got2[half, 0]) + (got2[half, 1] + got2[half, 2])

    for d in range(1, NZ):
        to = (z + d) % NZ
        send(sum2.at[to], got3.at[d - 1], 8, recv3.at[0], (to, y, c, x))

    @pl.when(c == 0)
    def _():
        wait_bytes(gotg2.at[pl.ds(0, 15)], recvg.at[1])
        tile = gotg2[0]
        for s in range(1, NZ):
            tile = tile + gotg2[s]
        gram[own] = tile
        for dy in range(NY):
            for dx in range(NX):
                for cc in range(2):
                    if (dy, dx, cc) != (0, 0, 0):
                        send(gram.at[own], gram.at[own], 9, recvg.at[2], (z, (y + dy) % NY, cc, (x + dx) % NX))
        wait_bytes(gram.at[pl.ds(0, 15)], recvg.at[2])

    @pl.when(c == 1)
    def _():
        wait_bytes(gram, recvg.at[2])

    wait_bytes(got3, recv3.at[0])
    total = sum2[z]
    for d in range(NZ - 1):
        total = total + got3[d]
    final[...] = total

    @pl.when(c == 0)
    def _():
        wait_bytes(gram0.at[pl.ds(0, 15)], send_sem.at[0])
        wait_bytes(gotg2.at[pl.ds(0, 15)], send_sem.at[3])
        wait_bytes(gotg1.at[pl.ds(0, 31)], send_sem.at[9])

    @pl.when(c == 1)
    def _():
        wait_bytes(gram0, send_sem.at[0])

    for half in range(2):
        wait_bytes(got0.at[half], send_sem.at[1 + half])
        wait_bytes(got1.at[half], send_sem.at[4 + half])
        wait_bytes(got2.at[half], send_sem.at[6 + half])
    wait_bytes(got3, send_sem.at[8])


def local(slab, sketch):
    rows, width = slab.shape
    rank = sketch.shape[1]
    total_rows = rows * lax.axis_size(("rows", "grp"))
    vmem = pl.BlockSpec(memory_space=pltpu.VMEM)
    tiles = lambda *lead: pltpu.VMEM((*lead, 8, 128), F32)
    first, gram, final = pl.pallas_call(
        exchange,
        out_shape=[
            jax.ShapeDtypeStruct((rows, rank), F32),
            jax.ShapeDtypeStruct((16, 8, 128), F32),
            jax.ShapeDtypeStruct((8, 128), F32),
        ],
        in_specs=[pl.BlockSpec(memory_space=pl.ANY)] * 2,
        out_specs=[vmem] * 3,
        scratch_shapes=[
            pltpu.VMEM((rows, width), BF16),
            pltpu.VMEM((width, rank), BF16),
            pltpu.VMEM((2 * rank, rows), BF16),
            tiles(2, 2, 4, 4, 8),
            tiles(2, 4, 4, 8),
            tiles(2, 3, 4, 8),
            tiles(2, 4, 8),
            tiles(2, 3, 8),
            tiles(16),
            tiles(15),
            tiles(16),
            tiles(32),
            tiles(16),
            pltpu.SemaphoreType.DMA((LOADS + 1,)),
            pltpu.SemaphoreType.DMA((10,)),
            pltpu.SemaphoreType.DMA((2,)),
            pltpu.SemaphoreType.DMA((2,)),
            pltpu.SemaphoreType.DMA((2,)),
            pltpu.SemaphoreType.DMA((1,)),
            pltpu.SemaphoreType.DMA((3,)),
        ],
        compiler_params=pltpu.CompilerParams(
            collective_id=0, has_side_effects=True, vmem_limit_bytes=56 * 2**20
        ),
    )(slab, sketch)
    lower = jnp.linalg.cholesky(gram.reshape(rank, rank))
    solve = lambda m: lax.linalg.triangular_solve(lower, m, left_side=False, lower=True, transpose_a=True)
    both = solve(jnp.concatenate([first, final], 0))
    basis = both[:rows] * jnp.sqrt(jnp.float32(total_rows))
    projected = (both[rows:] * jnp.sqrt(jnp.float32(width) / jnp.float32(total_rows))).astype(BF16)
    return (basis, projected)


def solution(mesh):
    return jax.shard_map(
        local,
        mesh=mesh,
        in_specs=(P(("rows", "grp"), None), P()),
        out_specs=(P(("rows", "grp"), None), P(("rows", "grp"), None)),
        check_vma=False,
    )
```

```python
import functools
import math

import jax
import jax.numpy as jnp
from jax import lax
from jax.experimental import pallas as pl
from jax.experimental.pallas import tpu as pltpu
from jax.sharding import PartitionSpec as P

MESH = pl.DeviceIdType.MESH
F32, BF16 = jnp.float32, jnp.bfloat16
NZ, NY, NX = 16, 4, 4
LOADS = 4


def place(z, y, c, x):
    return {"rows": (z * NY + y) * 2 + c, "grp": x}


def wait_bytes(ref, sem):
    pltpu.make_async_copy(ref, ref, sem).wait()


def lanes(tile, at):
    return jnp.broadcast_to(tile[:, at : at + 1], tile.shape)


def sublanes(tile, at):
    return jnp.broadcast_to(tile[at : at + 1, :], tile.shape)


def inverse_factor(gram):
    blocks = len(gram)
    shape = gram[0].shape
    row = lax.broadcasted_iota(jnp.int32, shape, 0)
    column = lax.broadcasted_iota(jnp.int32, shape, 1)
    left = list(gram)
    right = [jnp.where(column == row + 8 * i, 1.0, 0.0).astype(F32) for i in range(blocks)]
    out = []
    for b in range(blocks):
        tile, unit = left[b], right[b]
        cols = [lanes(tile, 8 * b + j) for j in range(8)]
        pivots = jnp.zeros(shape, F32)
        steps = []
        for j in range(8):
            pivot = sublanes(cols[j], j)
            pivots = jnp.where(row == j, pivot, pivots)
            inverse = 1.0 / pivot
            rest = {l: sublanes(cols[l], j) for l in range(j + 1, 8)}
            steps.append((inverse, sublanes(tile, j), sublanes(unit, j), rest))
            if j < 7:
                factor = jnp.where(row > j, cols[j] * inverse, 0.0)
                tile = tile - factor * steps[j][1]
                unit = unit - factor * steps[j][2]
                for l in rest:
                    cols[l] = cols[l] - factor * rest[l]
        out.append(unit * lax.rsqrt(pivots))
        for i in range(b + 1, blocks):
            cols = [lanes(left[i], 8 * b + j) for j in range(8)]
            for j, (inverse, tile_row, unit_row, rest) in enumerate(steps):
                factor = cols[j] * inverse
                left[i] = left[i] - factor * tile_row
                right[i] = right[i] - factor * unit_row
                for l in rest:
                    cols[l] = cols[l] - factor * rest[l]
    return out


def finish(basis_scale, projected_scale, first, inverse, final, basis, projected):
    def apply(matrix):
        return lax.dot_general(
            matrix, inverse[...], (((1,), (1,)), ((), ())), precision=lax.Precision.HIGHEST, preferred_element_type=F32
        )

    basis[...] = apply(first[...]) * basis_scale
    projected[...] = (apply(final[...]) * projected_scale).astype(BF16)


def exchange(
    slab, sketch, first, inverse, final,
    slab_v, sketch_v, first_t, part, got0, got1, sum1, got2, sum2, got3,
    gram0, gotg1, gotg2, gram,
    load_sem, send_sem, recv0, recv1, recv2, recv3, recvg,
):
    rows_at, x = lax.axis_index("rows"), lax.axis_index("grp")
    z, y, c = rows_at // (2 * NY), (rows_at // 2) % NY, rows_at % 2
    rows = slab.shape[0]
    step = rows // LOADS

    barrier = pltpu.get_barrier_semaphore()
    peers = [
        (z, (y + dy) % NY, (c + dc) % 2, (x + dx) % NX)
        for dy in range(NY) for dx in range(NX) for dc in range(2) if (dy, dx, dc) != (0, 0, 0)
    ] + [((z + d) % NZ, y, c, x) for d in range(1, NZ)]
    for peer in peers:
        pl.semaphore_signal(barrier, inc=1, device_id=place(*peer), device_id_type=MESH)

    sketch_copy = pltpu.make_async_copy(sketch, sketch_v, load_sem.at[LOADS])
    sketch_copy.start()
    loads = [
        pltpu.make_async_copy(slab.at[pl.ds(i * step, step)], slab_v.at[pl.ds(i * step, step)], load_sem.at[i])
        for i in range(LOADS)
    ]
    for load in loads:
        load.start()
    sketch_copy.wait()
    for i, load in enumerate(loads):
        load.wait()
        first[pl.ds(i * step, step), :] = jnp.dot(
            slab_v[pl.ds(i * step, step), :], sketch_v[...], preferred_element_type=F32
        )

    whole = first[...]
    whole_t = whole.T
    local = jnp.dot(whole_t, whole, precision=lax.Precision.HIGHEST, preferred_element_type=F32)
    for q in range(16):
        gram0[q] = local[8 * q : 8 * q + 8, :]
    high = whole_t.astype(BF16)
    low = (whole_t - high.astype(F32)).astype(BF16)
    first_t[...] = jnp.concatenate([high, low], 0)

    pl.semaphore_wait(barrier, len(peers))

    def send(src, dst, at, recv, peer):
        copy = pltpu.make_async_remote_copy(
            src_ref=src, dst_ref=dst, send_sem=send_sem.at[at], recv_sem=recv,
            device_id=place(*peer), device_id_type=MESH,
        )
        copy.start()

    own = y * NX + x
    for dy in range(NY):
        for dx in range(NX):
            ty, tx = (y + dy) % NY, (x + dx) % NX
            slot = (dy * NX + dx) * 2
            if (dy, dx) != (0, 0):
                send(gram0.at[ty * NX + tx], gotg1.at[slot + c], 0, recvg.at[0], (z, ty, 0, tx))

    @pl.when(c == 1)
    def _():
        send(gram0.at[own], gotg1.at[1], 0, recvg.at[0], (z, y, 0, x))

    @pl.when(c == 0)
    def _():
        gotg1[0] = gram0[own]

    wide = 512
    for j in range(8):
        both = jnp.dot(first_t[...], slab_v[:, j * wide : (j + 1) * wide], preferred_element_type=F32)
        sums = both[:128] + both[128:]
        for k in range(4):
            block = sums[:, k * 128 : (k + 1) * 128].T
            at_z, half = (2 * j + k // 2), j // 4
            for yl in range(2):
                for cc in range(2):
                    for xx in range(4):
                        row = ((yl * 2 + cc) * 4 + xx) * 8
                        yy = 2 * (k % 2) + yl
                        a, b = (xx, yy) if half == 0 else (yy, xx)
                        part[cc, half, a, b, at_z % 8] = block[row : row + 8, :]
        if j % 4 == 3:
            half = j // 4
            send(part.at[1 - c, half], got0.at[half], 1 + half, recv0.at[half], (z, y, 1 - c, x))

    @pl.when(c == 0)
    def _():
        wait_bytes(gotg1.at[pl.ds(0, 31)], recvg.at[0])
        tile = gotg1[0]
        for s in range(1, 32):
            tile = tile + gotg1[s]
        gotg2[z] = tile
        for d in range(1, NZ):
            send(gotg2.at[z], gotg2.at[z], 3, recvg.at[1], ((z + d) % NZ, y, c, x))

    def peer_of(half, phase, d):
        if (half + phase) % 2 == 0:
            return (z, y, c, (x + d) % NX)
        return (z, (y + d) % NY, c, x)

    def index_of(half, phase, d):
        return (x + d) % NX if (half + phase) % 2 == 0 else (y + d) % NY

    for half in range(2):
        wait_bytes(got0.at[half], recv0.at[half])
        for d in (2, 1, 3, 0):
            a = index_of(half, 0, d)
            part[c, half, a] = part[c, half, a] + got0[half, a]
            if d:
                send(part.at[c, half, a], got1.at[half, d - 1], 4 + half, recv1.at[half], peer_of(half, 0, d))

    for half in range(2):
        wait_bytes(got1.at[half], recv1.at[half])
        a = index_of(half, 0, 0)
        for d in (2, 1, 3, 0):
            b = index_of(half, 1, d)
            sum1[half, b] = (part[c, half, a, b] + got1[half, 0, b]) + (got1[half, 1, b] + got1[half, 2, b])
            if d:
                send(sum1.at[half, b], got2.at[half, d - 1], 6 + half, recv2.at[half], peer_of(half, 1, d))

    for half in range(2):
        wait_bytes(got2.at[half], recv2.at[half])
        b = index_of(half, 1, 0)
        sum2[pl.ds(8 * half, 8)] = (sum1[half, b] + got2[half, 0]) + (got2[half, 1] + got2[half, 2])

    for d in range(1, NZ):
        to = (z + d) % NZ
        send(sum2.at[to], got3.at[d - 1], 8, recv3.at[0], (to, y, c, x))

    @pl.when(c == 0)
    def _():
        wait_bytes(gotg2.at[pl.ds(0, 15)], recvg.at[1])
        tile = gotg2[0]
        for s in range(1, NZ):
            tile = tile + gotg2[s]
        gram[own] = tile
        for dy in range(NY):
            for dx in range(NX):
                for cc in range(2):
                    if (dy, dx, cc) != (0, 0, 0):
                        send(gram.at[own], gram.at[own], 9, recvg.at[2], (z, (y + dy) % NY, cc, (x + dx) % NX))
        wait_bytes(gram.at[pl.ds(0, 15)], recvg.at[2])

    @pl.when(c == 1)
    def _():
        wait_bytes(gram, recvg.at[2])

    for i, tile in enumerate(inverse_factor([gram[q] for q in range(16)])):
        inverse[8 * i : 8 * i + 8, :] = tile

    wait_bytes(got3, recv3.at[0])
    total = sum2[z]
    for d in range(NZ - 1):
        total = total + got3[d]
    final[...] = total

    @pl.when(c == 0)
    def _():
        wait_bytes(gram0.at[pl.ds(0, 15)], send_sem.at[0])
        wait_bytes(gotg2.at[pl.ds(0, 15)], send_sem.at[3])
        wait_bytes(gotg1.at[pl.ds(0, 31)], send_sem.at[9])

    @pl.when(c == 1)
    def _():
        wait_bytes(gram0, send_sem.at[0])

    for half in range(2):
        wait_bytes(got0.at[half], send_sem.at[1 + half])
        wait_bytes(got1.at[half], send_sem.at[4 + half])
        wait_bytes(got2.at[half], send_sem.at[6 + half])
    wait_bytes(got3, send_sem.at[8])


def local(slab, sketch):
    rows, width = slab.shape
    rank = sketch.shape[1]
    total_rows = rows * lax.axis_size(("rows", "grp"))
    vmem = pl.BlockSpec(memory_space=pltpu.VMEM)
    tiles = lambda *lead: pltpu.VMEM((*lead, 8, 128), F32)
    first, inverse, final = pl.pallas_call(
        exchange,
        out_shape=[
            jax.ShapeDtypeStruct((rows, rank), F32),
            jax.ShapeDtypeStruct((rank, rank), F32),
            jax.ShapeDtypeStruct((8, 128), F32),
        ],
        in_specs=[pl.BlockSpec(memory_space=pl.ANY)] * 2,
        out_specs=[vmem] * 3,
        scratch_shapes=[
            pltpu.VMEM((rows, width), BF16),
            pltpu.VMEM((width, rank), BF16),
            pltpu.VMEM((2 * rank, rows), BF16),
            tiles(2, 2, 4, 4, 8),
            tiles(2, 4, 4, 8),
            tiles(2, 3, 4, 8),
            tiles(2, 4, 8),
            tiles(2, 3, 8),
            tiles(16),
            tiles(15),
            tiles(16),
            tiles(32),
            tiles(16),
            tiles(16),
            pltpu.SemaphoreType.DMA((LOADS + 1,)),
            pltpu.SemaphoreType.DMA((10,)),
            pltpu.SemaphoreType.DMA((2,)),
            pltpu.SemaphoreType.DMA((2,)),
            pltpu.SemaphoreType.DMA((2,)),
            pltpu.SemaphoreType.DMA((1,)),
            pltpu.SemaphoreType.DMA((3,)),
        ],
        compiler_params=pltpu.CompilerParams(
            collective_id=0, has_side_effects=True, vmem_limit_bytes=56 * 2**20
        ),
    )(slab, sketch)
    basis, projected = pl.pallas_call(
        functools.partial(finish, math.sqrt(total_rows), math.sqrt(width / total_rows)),
        out_shape=[jax.ShapeDtypeStruct((rows, rank), F32), jax.ShapeDtypeStruct((8, 128), BF16)],
    )(first, inverse, final)
    return (basis, projected)


def solution(mesh):
    return jax.shard_map(
        local,
        mesh=mesh,
        in_specs=(P(("rows", "grp"), None), P()),
        out_specs=(P(("rows", "grp"), None), P(("rows", "grp"), None)),
        check_vma=False,
    )
```

```python
import functools
import math

import jax
import jax.numpy as jnp
from jax import lax
from jax.experimental import pallas as pl
from jax.experimental.pallas import tpu as pltpu
from jax.sharding import PartitionSpec as P

MESH = pl.DeviceIdType.MESH
F32, BF16 = jnp.float32, jnp.bfloat16
NZ, NY, NX = 16, 4, 4
LOADS = 4


def place(z, y, c, x):
    return {"rows": (z * NY + y) * 2 + c, "grp": x}


def wait_bytes(ref, sem):
    pltpu.make_async_copy(ref, ref, sem).wait()


def lanes(tile, at):
    return jnp.broadcast_to(tile[:, at : at + 1], tile.shape)


def sublanes(tile, at):
    return jnp.broadcast_to(tile[at : at + 1, :], tile.shape)


def inverse_factor(gram):
    blocks = len(gram)
    shape = gram[0].shape
    row = lax.broadcasted_iota(jnp.int32, shape, 0)
    column = lax.broadcasted_iota(jnp.int32, shape, 1)
    left = list(gram)
    right = [jnp.where(column == row + 8 * i, 1.0, 0.0).astype(F32) for i in range(blocks)]
    out = []
    for b in range(blocks):
        tile, unit = left[b], right[b]
        cols = [lanes(tile, 8 * b + j) for j in range(8)]
        pivots = jnp.zeros(shape, F32)
        steps = []
        for j in range(8):
            pivot = sublanes(cols[j], j)
            pivots = jnp.where(row == j, pivot, pivots)
            inverse = 1.0 / pivot
            rest = {l: sublanes(cols[l], j) for l in range(j + 1, 8)}
            steps.append((inverse, sublanes(tile, j), sublanes(unit, j), rest))
            if j < 7:
                factor = jnp.where(row > j, cols[j] * inverse, 0.0)
                tile = tile - factor * steps[j][1]
                unit = unit - factor * steps[j][2]
                for l in rest:
                    cols[l] = cols[l] - factor * rest[l]
        out.append(unit * lax.rsqrt(pivots))
        for i in range(b + 1, blocks):
            cols = [lanes(left[i], 8 * b + j) for j in range(8)]
            for j, (inverse, tile_row, unit_row, rest) in enumerate(steps):
                factor = cols[j] * inverse
                left[i] = left[i] - factor * tile_row
                right[i] = right[i] - factor * unit_row
                for l in rest:
                    cols[l] = cols[l] - factor * rest[l]
    return out


def finish(basis_scale, projected_scale, first, inverse, final, basis, projected):
    def apply(matrix):
        return lax.dot_general(
            matrix, inverse[...], (((1,), (1,)), ((), ())), precision=lax.Precision.HIGHEST, preferred_element_type=F32
        )

    basis[...] = apply(first[...]) * basis_scale
    projected[...] = (apply(final[...]) * projected_scale).astype(BF16)


def exchange(
    slab, sketch, first_out, inverse, final,
    slab_v, sketch_v, first, first_t, part, got0, got1, sum1, got2, sum2, got3,
    gram0, gotg1, gotg2, gram,
    load_sem, send_sem, recv0, recv1, recv2, recv3, recvg, ready,
):
    rows_at, x = lax.axis_index("rows"), lax.axis_index("grp")
    z, y, c = rows_at // (2 * NY), (rows_at // 2) % NY, rows_at % 2
    rows = slab.shape[0]
    step = rows // LOADS

    def send(src, dst, at, recv, peer):
        pltpu.make_async_remote_copy(
            src_ref=src, dst_ref=dst, send_sem=send_sem.at[at], recv_sem=recv,
            device_id=place(*peer), device_id_type=MESH,
        ).start()

    def hops(dy, dx):
        return min(dy, NY - dy) + min(dx, NX - dx)

    chips = sorted(((dy, dx) for dy in range(NY) for dx in range(NX)), key=lambda d: -hops(*d))

    sketch_copy = pltpu.make_async_copy(sketch, sketch_v, load_sem.at[LOADS])
    sketch_copy.start()
    loads = [
        pltpu.make_async_copy(slab.at[pl.ds(i * step, step)], slab_v.at[pl.ds(i * step, step)], load_sem.at[i])
        for i in range(LOADS)
    ]
    for load in loads:
        load.start()

    barrier = pltpu.get_barrier_semaphore()
    peers = [((z + d) % NZ, y, c, x) for d in (4, 12, 3, 13, 2, 14, 1, 15)] + [
        (z, (y + dy) % NY, (c + dc) % 2, (x + dx) % NX)
        for dy, dx in chips for dc in range(2) if (dy, dx, dc) != (0, 0, 0)
    ]
    for peer in peers:
        pl.semaphore_signal(barrier, inc=1, device_id=place(*peer), device_id_type=MESH)

    sketch_copy.wait()
    for i, load in enumerate(loads):
        load.wait()
        first[pl.ds(i * step, step), :] = jnp.dot(
            slab_v[pl.ds(i * step, step), :], sketch_v[...], preferred_element_type=F32
        )
    store = pltpu.make_async_copy(first, first_out, load_sem.at[LOADS + 1])
    store.start()

    whole = first[...]
    whole_t = whole.T
    local = jnp.dot(whole_t, whole, precision=lax.Precision.HIGHEST, preferred_element_type=F32)
    for q in range(16):
        gram0[q] = local[8 * q : 8 * q + 8, :]
    high = whole_t.astype(BF16)
    low = (whole_t - high.astype(F32)).astype(BF16)
    first_t[...] = jnp.concatenate([high, low], 0)

    def product(half):
        wide = 512
        for j in range(4 * half, 4 * half + 4):
            both = jnp.dot(first_t[...], slab_v[:, j * wide : (j + 1) * wide], preferred_element_type=F32)
            sums = both[:128] + both[128:]
            for k in range(4):
                block = sums[:, k * 128 : (k + 1) * 128].T
                at_z = 2 * j + k // 2
                for yl in range(2):
                    for cc in range(2):
                        for xx in range(4):
                            row = ((yl * 2 + cc) * 4 + xx) * 8
                            yy = 2 * (k % 2) + yl
                            a, b = (xx, yy) if half == 0 else (yy, xx)
                            part[cc, half, a, b, at_z % 8] = block[row : row + 8, :]

    def to_core(half):
        send(part.at[1 - c, half], got0.at[half], 1 + half, recv0.at[half], (z, y, 1 - c, x))

    product(0)

    pl.semaphore_wait(barrier, len(peers))
    for d in (4, 12):
        pl.semaphore_signal(ready, inc=1, device_id=place((z + d) % NZ, y, c, x), device_id_type=MESH)

    own = y * NX + x
    for dy, dx in chips:
        ty, tx = (y + dy) % NY, (x + dx) % NX
        if (dy, dx) != (0, 0):
            send(gram0.at[ty * NX + tx], gotg1.at[(dy * NX + dx) * 2 + c], 0, recvg.at[0], (z, ty, 0, tx))

    @pl.when(c == 1)
    def _():
        send(gram0.at[own], gotg1.at[1], 0, recvg.at[0], (z, y, 0, x))

    @pl.when(c == 0)
    def _():
        gotg1[0] = gram0[own]

    to_core(0)
    product(1)
    to_core(1)

    def peer_of(half, phase, d):
        if (half + phase) % 2 == 0:
            return (z, y, c, (x + d) % NX)
        return (z, (y + d) % NY, c, x)

    def index_of(half, phase, d):
        return (x + d) % NX if (half + phase) % 2 == 0 else (y + d) % NY

    for half in range(2):
        wait_bytes(got0.at[half], recv0.at[half])
        for d in (2, 1, 3, 0):
            a = index_of(half, 0, d)
            part[c, half, a] = part[c, half, a] + got0[half, a]
            if d:
                send(part.at[c, half, a], got1.at[half, d - 1], 4 + half, recv1.at[half], peer_of(half, 0, d))

    pl.semaphore_wait(ready, 2)

    @pl.when(c == 0)
    def _():
        wait_bytes(gotg1.at[pl.ds(0, 31)], recvg.at[0])
        tile = gotg1[0]
        for s in range(1, 32):
            tile = tile + gotg1[s]
        gotg2[z] = tile
        for to in range(NZ):
            @pl.when(z != to)
            def _():
                send(gotg2.at[z], gotg2.at[z], 3, recvg.at[1], (to, y, c, x))

    for half in range(2):
        wait_bytes(got1.at[half], recv1.at[half])
        a = index_of(half, 0, 0)
        for d in (2, 1, 3, 0):
            b = index_of(half, 1, d)
            sum1[half, b] = (part[c, half, a, b] + got1[half, 0, b]) + (got1[half, 1, b] + got1[half, 2, b])
            if d:
                send(sum1.at[half, b], got2.at[half, d - 1], 6 + half, recv2.at[half], peer_of(half, 1, d))

    @pl.when(c == 0)
    def _():
        wait_bytes(gotg2.at[pl.ds(0, 15)], recvg.at[1])
        tile = gotg2[0]
        for s in range(1, NZ):
            tile = tile + gotg2[s]
        gram[own] = tile
        for dy, dx in chips:
            for cc in range(2):
                if (dy, dx, cc) != (0, 0, 0):
                    send(gram.at[own], gram.at[own], 9, recvg.at[2], (z, (y + dy) % NY, cc, (x + dx) % NX))

    for half in range(2):
        wait_bytes(got2.at[half], recv2.at[half])
        b = index_of(half, 1, 0)
        sum2[pl.ds(8 * half, 8)] = (sum1[half, b] + got2[half, 0]) + (got2[half, 1] + got2[half, 2])
        for to in range(8 * half, 8 * half + 8):
            @pl.when(z != to)
            def _():
                send(sum2.at[to], got3.at[z], 8, recv3.at[0], (to, y, c, x))

    @pl.when(c == 0)
    def _():
        wait_bytes(gram.at[pl.ds(0, 15)], recvg.at[2])

    @pl.when(c == 1)
    def _():
        wait_bytes(gram, recvg.at[2])

    for i, tile in enumerate(inverse_factor([gram[q] for q in range(16)])):
        inverse[8 * i : 8 * i + 8, :] = tile

    got3[z] = sum2[z]
    wait_bytes(got3.at[pl.ds(0, 15)], recv3.at[0])
    total = got3[0]
    for s in range(1, NZ):
        total = total + got3[s]
    final[...] = total

    @pl.when(c == 0)
    def _():
        wait_bytes(gram0.at[pl.ds(0, 15)], send_sem.at[0])
        wait_bytes(gotg2.at[pl.ds(0, 15)], send_sem.at[3])
        wait_bytes(gotg1.at[pl.ds(0, 31)], send_sem.at[9])

    @pl.when(c == 1)
    def _():
        wait_bytes(gram0, send_sem.at[0])

    for half in range(2):
        wait_bytes(got0.at[half], send_sem.at[1 + half])
        wait_bytes(got1.at[half], send_sem.at[4 + half])
        wait_bytes(got2.at[half], send_sem.at[6 + half])
    wait_bytes(got3.at[pl.ds(0, 15)], send_sem.at[8])
    store.wait()


def local(slab, sketch):
    rows, width = slab.shape
    rank = sketch.shape[1]
    total_rows = rows * lax.axis_size(("rows", "grp"))
    vmem = pl.BlockSpec(memory_space=pltpu.VMEM)
    tiles = lambda *lead: pltpu.VMEM((*lead, 8, 128), F32)
    first, inverse, final = pl.pallas_call(
        exchange,
        out_shape=[
            jax.ShapeDtypeStruct((rows, rank), F32),
            jax.ShapeDtypeStruct((rank, rank), F32),
            jax.ShapeDtypeStruct((8, 128), F32),
        ],
        in_specs=[pl.BlockSpec(memory_space=pl.ANY)] * 2,
        out_specs=[pl.BlockSpec(memory_space=pl.ANY), vmem, vmem],
        scratch_shapes=[
            pltpu.VMEM((rows, width), BF16),
            pltpu.VMEM((width, rank), BF16),
            pltpu.VMEM((rows, rank), F32),
            pltpu.VMEM((2 * rank, rows), BF16),
            tiles(2, 2, 4, 4, 8),
            tiles(2, 4, 4, 8),
            tiles(2, 3, 4, 8),
            tiles(2, 4, 8),
            tiles(2, 3, 8),
            tiles(16),
            tiles(16),
            tiles(16),
            tiles(32),
            tiles(16),
            tiles(16),
            pltpu.SemaphoreType.DMA((LOADS + 2,)),
            pltpu.SemaphoreType.DMA((10,)),
            pltpu.SemaphoreType.DMA((2,)),
            pltpu.SemaphoreType.DMA((2,)),
            pltpu.SemaphoreType.DMA((2,)),
            pltpu.SemaphoreType.DMA((1,)),
            pltpu.SemaphoreType.DMA((3,)),
            pltpu.SemaphoreType.REGULAR,
        ],
        compiler_params=pltpu.CompilerParams(
            collective_id=0, has_side_effects=True, vmem_limit_bytes=56 * 2**20
        ),
    )(slab, sketch)
    basis, projected = pl.pallas_call(
        functools.partial(finish, math.sqrt(total_rows), math.sqrt(width / total_rows)),
        out_shape=[jax.ShapeDtypeStruct((rows, rank), F32), jax.ShapeDtypeStruct((8, 128), BF16)],
    )(first, inverse, final)
    return (basis, projected)


def solution(mesh):
    return jax.shard_map(
        local,
        mesh=mesh,
        in_specs=(P(("rows", "grp"), None), P()),
        out_specs=(P(("rows", "grp"), None), P(("rows", "grp"), None)),
        check_vma=False,
    )
```

```python
import functools
import math

import jax
import jax.numpy as jnp
from jax import lax
from jax.experimental import pallas as pl
from jax.experimental.pallas import tpu as pltpu
from jax.sharding import PartitionSpec as P

MESH = pl.DeviceIdType.MESH
F32, BF16 = jnp.float32, jnp.bfloat16
NZ, NY, NX = 16, 4, 4
LOADS = 4


def place(z, y, c, x):
    return {"rows": (z * NY + y) * 2 + c, "grp": x}


def wait_bytes(ref, sem):
    pltpu.make_async_copy(ref, ref, sem).wait()


def lanes(tile, at):
    return jnp.broadcast_to(tile[:, at : at + 1], tile.shape)


def sublanes(tile, at):
    return jnp.broadcast_to(tile[at : at + 1, :], tile.shape)


def inverse_factor(gram):
    blocks = len(gram)
    shape = gram[0].shape
    row = lax.broadcasted_iota(jnp.int32, shape, 0)
    column = lax.broadcasted_iota(jnp.int32, shape, 1)
    left = list(gram)
    right = [jnp.where(column == row + 8 * i, 1.0, 0.0).astype(F32) for i in range(blocks)]
    out = []
    for b in range(blocks):
        tile, unit = left[b], right[b]
        cols = [lanes(tile, 8 * b + j) for j in range(8)]
        pivots = jnp.zeros(shape, F32)
        steps = []
        for j in range(8):
            pivot = sublanes(cols[j], j)
            pivots = jnp.where(row == j, pivot, pivots)
            inverse = 1.0 / pivot
            rest = {l: sublanes(cols[l], j) for l in range(j + 1, 8)}
            steps.append((inverse, sublanes(tile, j), sublanes(unit, j), rest))
            if j < 7:
                factor = jnp.where(row > j, cols[j] * inverse, 0.0)
                tile = tile - factor * steps[j][1]
                unit = unit - factor * steps[j][2]
                for l in rest:
                    cols[l] = cols[l] - factor * rest[l]
        out.append(unit * lax.rsqrt(pivots))
        for i in range(b + 1, blocks):
            cols = [lanes(left[i], 8 * b + j) for j in range(8)]
            for j, (inverse, tile_row, unit_row, rest) in enumerate(steps):
                factor = cols[j] * inverse
                left[i] = left[i] - factor * tile_row
                right[i] = right[i] - factor * unit_row
                for l in rest:
                    cols[l] = cols[l] - factor * rest[l]
    return out


def finish(basis_scale, projected_scale, first, inverse, final, basis, projected):
    def apply(matrix):
        return lax.dot_general(
            matrix, inverse[...], (((1,), (1,)), ((), ())), precision=lax.Precision.HIGHEST, preferred_element_type=F32
        )

    basis[...] = apply(first[...]) * basis_scale
    projected[...] = (apply(final[...]) * projected_scale).astype(BF16)


def exchange(
    slab, sketch, first, inverse, final,
    slab_v, sketch_v, first_t, part, got0, got1, sum1, got2, sum2, got3,
    gram0, gotg1, gotg2, gram,
    load_sem, send_sem, recv0, recv1, recv2, recv3, recvg, ready,
):
    rows_at, x = lax.axis_index("rows"), lax.axis_index("grp")
    z, y, c = rows_at // (2 * NY), (rows_at // 2) % NY, rows_at % 2
    rows = slab.shape[0]
    step = rows // LOADS

    def send(src, dst, at, recv, peer):
        pltpu.make_async_remote_copy(
            src_ref=src, dst_ref=dst, send_sem=send_sem.at[at], recv_sem=recv,
            device_id=place(*peer), device_id_type=MESH,
        ).start()

    def hops(dy, dx):
        return min(dy, NY - dy) + min(dx, NX - dx)

    chips = sorted(((dy, dx) for dy in range(NY) for dx in range(NX)), key=lambda d: -hops(*d))

    sketch_copy = pltpu.make_async_copy(sketch, sketch_v, load_sem.at[LOADS])
    sketch_copy.start()
    loads = [
        pltpu.make_async_copy(slab.at[pl.ds(i * step, step)], slab_v.at[pl.ds(i * step, step)], load_sem.at[i])
        for i in range(LOADS)
    ]
    for load in loads:
        load.start()

    barrier = pltpu.get_barrier_semaphore()
    peers = [((z + d) % NZ, y, c, x) for d in (4, 12, 3, 13, 2, 14, 1, 15)] + [
        (z, (y + dy) % NY, (c + dc) % 2, (x + dx) % NX)
        for dy, dx in chips for dc in range(2) if (dy, dx, dc) != (0, 0, 0)
    ]
    for peer in peers:
        pl.semaphore_signal(barrier, inc=1, device_id=place(*peer), device_id_type=MESH)

    sketch_copy.wait()
    for i, load in enumerate(loads):
        load.wait()
        first[pl.ds(i * step, step), :] = jnp.dot(
            slab_v[pl.ds(i * step, step), :], sketch_v[...], preferred_element_type=F32
        )

    whole = first[...]
    whole_t = whole.T
    local = jnp.dot(whole_t, whole, precision=lax.Precision.HIGHEST, preferred_element_type=F32)
    for q in range(16):
        gram0[q] = local[8 * q : 8 * q + 8, :]
    high = whole_t.astype(BF16)
    low = (whole_t - high.astype(F32)).astype(BF16)
    first_t[...] = jnp.concatenate([high, low], 0)

    def product(j):
        both = jnp.dot(first_t[...], slab_v[:, j * 512 : (j + 1) * 512], preferred_element_type=F32)
        sums = both[:128] + both[128:]
        for k in range(4):
            block = sums[:, k * 128 : (k + 1) * 128].T
            for yl in range(2):
                for cc in range(2):
                    for xx in range(4):
                        row = ((yl * 2 + cc) * 4 + xx) * 8
                        yy = 2 * (k % 2) + yl
                        a, b = (xx, yy) if j % 2 == 0 else (yy, xx)
                        part[cc, j, a, b, k // 2] = block[row : row + 8, :]

    def peer_of(j, phase, d):
        if (j + phase) % 2 == 0:
            return (z, y, c, (x + d) % NX)
        return (z, (y + d) % NY, c, x)

    def index_of(j, phase, d):
        return (x + d) % NX if (j + phase) % 2 == 0 else (y + d) % NY

    def to_core(j):
        send(part.at[1 - c, j], got0.at[j], 1, recv0.at[j], (z, y, 1 - c, x))

    def to_first_axis(j):
        wait_bytes(got0.at[j], recv0.at[j])
        for d in (2, 1, 3, 0):
            a = index_of(j, 0, d)
            part[c, j, a] = part[c, j, a] + got0[j, a]
            if d:
                send(part.at[c, j, a], got1.at[j, d - 1], 2, recv1.at[j], peer_of(j, 0, d))

    def to_second_axis(j):
        wait_bytes(got1.at[j], recv1.at[j])
        a = index_of(j, 0, 0)
        for d in (2, 1, 3, 0):
            b = index_of(j, 1, d)
            sum1[j, b] = (part[c, j, a, b] + got1[j, 0, b]) + (got1[j, 1, b] + got1[j, 2, b])
            if d:
                send(sum1.at[j, b], got2.at[j, d - 1], 4, recv2.at[j], peer_of(j, 1, d))

    def to_planes(j):
        wait_bytes(got2.at[j], recv2.at[j])
        b = index_of(j, 1, 0)
        sum2[pl.ds(2 * j, 2)] = (sum1[j, b] + got2[j, 0]) + (got2[j, 1] + got2[j, 2])
        for to in range(2 * j, 2 * j + 2):
            @pl.when(z != to)
            def _():
                send(sum2.at[to], got3.at[z], 5, recv3.at[0], (to, y, c, x))


    pl.semaphore_wait(barrier, len(peers))
    for d in (4, 12):
        pl.semaphore_signal(ready, inc=1, device_id=place((z + d) % NZ, y, c, x), device_id_type=MESH)

    own = y * NX + x
    for dy, dx in chips:
        ty, tx = (y + dy) % NY, (x + dx) % NX
        if (dy, dx) != (0, 0):
            send(gram0.at[ty * NX + tx], gotg1.at[(dy * NX + dx) * 2 + c], 0, recvg.at[0], (z, ty, 0, tx))

    @pl.when(c == 1)
    def _():
        send(gram0.at[own], gotg1.at[1], 0, recvg.at[0], (z, y, 0, x))

    @pl.when(c == 0)
    def _():
        gotg1[0] = gram0[own]

    for j in range(8):
        product(j)
        to_core(j)
        if j >= 4:
            to_first_axis(j - 4)

    for j in range(4, 4):
        to_first_axis(j)

    pl.semaphore_wait(ready, 2)

    @pl.when(c == 0)
    def _():
        wait_bytes(gotg1.at[pl.ds(0, 31)], recvg.at[0])
        tile = gotg1[0]
        for s in range(1, 32):
            tile = tile + gotg1[s]
        gotg2[z] = tile
        for to in range(NZ):
            @pl.when(z != to)
            def _():
                send(gotg2.at[z], gotg2.at[z], 3, recvg.at[1], (to, y, c, x))

    for j in range(4, 8):
        to_first_axis(j)

    for j in range(8):
        to_second_axis(j)
    for j in range(4):
        to_planes(j)

    @pl.when(c == 0)
    def _():
        wait_bytes(gotg2.at[pl.ds(0, 15)], recvg.at[1])
        tile = gotg2[0]
        for s in range(1, NZ):
            tile = tile + gotg2[s]
        gram[own] = tile
        for dy, dx in chips:
            for cc in range(2):
                if (dy, dx, cc) != (0, 0, 0):
                    send(gram.at[own], gram.at[own], 6, recvg.at[2], (z, (y + dy) % NY, cc, (x + dx) % NX))

    for j in range(4, 8):
        to_planes(j)

    @pl.when(c == 0)
    def _():
        wait_bytes(gram.at[pl.ds(0, 15)], recvg.at[2])

    @pl.when(c == 1)
    def _():
        wait_bytes(gram, recvg.at[2])

    for i, tile in enumerate(inverse_factor([gram[q] for q in range(16)])):
        inverse[8 * i : 8 * i + 8, :] = tile

    got3[z] = sum2[z]
    wait_bytes(got3.at[pl.ds(0, 15)], recv3.at[0])
    total = got3[0]
    for s in range(1, NZ):
        total = total + got3[s]
    final[...] = total

    @pl.when(c == 0)
    def _():
        wait_bytes(gram0.at[pl.ds(0, 15)], send_sem.at[0])
        wait_bytes(gotg2.at[pl.ds(0, 15)], send_sem.at[3])
        wait_bytes(gotg1.at[pl.ds(0, 31)], send_sem.at[6])

    @pl.when(c == 1)
    def _():
        wait_bytes(gram0, send_sem.at[0])

    wait_bytes(got0, send_sem.at[1])
    wait_bytes(got1, send_sem.at[2])
    wait_bytes(got2, send_sem.at[4])
    wait_bytes(got3.at[pl.ds(0, 15)], send_sem.at[5])


def local(slab, sketch):
    rows, width = slab.shape
    rank = sketch.shape[1]
    total_rows = rows * lax.axis_size(("rows", "grp"))
    vmem = pl.BlockSpec(memory_space=pltpu.VMEM)
    tiles = lambda *lead: pltpu.VMEM((*lead, 8, 128), F32)
    first, inverse, final = pl.pallas_call(
        exchange,
        out_shape=[pltpu.VMEM((rows, rank), F32), pltpu.VMEM((rank, rank), F32), pltpu.VMEM((8, 128), F32)],
        in_specs=[pl.BlockSpec(memory_space=pl.ANY)] * 2,
        out_specs=[vmem] * 3,
        scratch_shapes=[
            pltpu.VMEM((rows, width), BF16),
            pltpu.VMEM((width, rank), BF16),
            pltpu.VMEM((2 * rank, rows), BF16),
            tiles(2, 8, 4, 4, 2),
            tiles(8, 4, 4, 2),
            tiles(8, 3, 4, 2),
            tiles(8, 4, 2),
            tiles(8, 3, 2),
            tiles(16),
            tiles(16),
            tiles(16),
            tiles(32),
            tiles(16),
            tiles(16),
            pltpu.SemaphoreType.DMA((LOADS + 1,)),
            pltpu.SemaphoreType.DMA((7,)),
            pltpu.SemaphoreType.DMA((8,)),
            pltpu.SemaphoreType.DMA((8,)),
            pltpu.SemaphoreType.DMA((8,)),
            pltpu.SemaphoreType.DMA((1,)),
            pltpu.SemaphoreType.DMA((3,)),
            pltpu.SemaphoreType.REGULAR,
        ],
        compiler_params=pltpu.CompilerParams(
            collective_id=0, has_side_effects=True, vmem_limit_bytes=24 * 2**20
        ),
    )(*(pltpu.with_memory_space_constraint(array, pltpu.HBM) for array in (slab, sketch)))
    basis, projected = pl.pallas_call(
        functools.partial(finish, math.sqrt(total_rows), math.sqrt(width / total_rows)),
        out_shape=[jax.ShapeDtypeStruct((rows, rank), F32), jax.ShapeDtypeStruct((8, 128), BF16)],
        compiler_params=pltpu.CompilerParams(vmem_limit_bytes=8 * 2**20),
    )(*(pltpu.with_memory_space_constraint(array, pltpu.VMEM) for array in (first, inverse, final)))
    return (basis, projected)


def solution(mesh):
    return jax.shard_map(
        local,
        mesh=mesh,
        in_specs=(P(("rows", "grp"), None), P()),
        out_specs=(P(("rows", "grp"), None), P(("rows", "grp"), None)),
        check_vma=False,
    )
```

```python
import functools
import math

import jax
import jax.numpy as jnp
from jax import lax
from jax.experimental import pallas as pl
from jax.experimental.pallas import tpu as pltpu
from jax.sharding import PartitionSpec as P

MESH = pl.DeviceIdType.MESH
F32, BF16 = jnp.float32, jnp.bfloat16
NZ, NY, NX = 16, 4, 4
LOADS = 4


def place(z, y, c, x):
    return {"rows": (z * NY + y) * 2 + c, "grp": x}


def wait_bytes(ref, sem):
    pltpu.make_async_copy(ref, ref, sem).wait()


def lanes(tile, at):
    return jnp.broadcast_to(tile[:, at : at + 1], tile.shape)


def sublanes(tile, at):
    return jnp.broadcast_to(tile[at : at + 1, :], tile.shape)


def inverse_factor(gram):
    blocks = len(gram)
    shape = gram[0].shape
    row = lax.broadcasted_iota(jnp.int32, shape, 0)
    column = lax.broadcasted_iota(jnp.int32, shape, 1)
    left = list(gram)
    right = [jnp.where(column == row + 8 * i, 1.0, 0.0).astype(F32) for i in range(blocks)]
    out = []
    for b in range(blocks):
        tile, unit = left[b], right[b]
        cols = [lanes(tile, 8 * b + j) for j in range(8)]
        pivots = jnp.zeros(shape, F32)
        steps = []
        for j in range(8):
            pivot = sublanes(cols[j], j)
            pivots = jnp.where(row == j, pivot, pivots)
            inverse = 1.0 / pivot
            rest = {l: sublanes(cols[l], j) for l in range(j + 1, 8)}
            steps.append((inverse, sublanes(tile, j), sublanes(unit, j), rest))
            if j < 7:
                factor = jnp.where(row > j, cols[j] * inverse, 0.0)
                tile = tile - factor * steps[j][1]
                unit = unit - factor * steps[j][2]
                for l in rest:
                    cols[l] = cols[l] - factor * rest[l]
        out.append(unit * lax.rsqrt(pivots))
        for i in range(b + 1, blocks):
            cols = [lanes(left[i], 8 * b + j) for j in range(8)]
            for j, (inverse, tile_row, unit_row, rest) in enumerate(steps):
                factor = cols[j] * inverse
                left[i] = left[i] - factor * tile_row
                right[i] = right[i] - factor * unit_row
                for l in rest:
                    cols[l] = cols[l] - factor * rest[l]
    return out


def finish(basis_scale, projected_scale, first, inverse, final, basis, projected):
    def apply(matrix):
        return lax.dot_general(
            matrix, inverse[...], (((1,), (1,)), ((), ())), precision=lax.Precision.HIGHEST, preferred_element_type=F32
        )

    basis[...] = apply(first[...]) * basis_scale
    projected[...] = (apply(final[...]) * projected_scale).astype(BF16)


def owner_of(tile):
    at = tile // 2 + 1
    return (at // 3 + 3) % NY, tile % 2, (at % 3 + 3) % NX


def exchange(
    slab, sketch, first, inverse, final,
    slab_v, sketch_v, first_t, part, got0, got1, sum1, got2, sum2, got3,
    gram0, gotg1, gotg2, gram,
    load_sem, send_sem, recv0, recv1, recv2, recv3, recvg, ready,
):
    rows_at, x = lax.axis_index("rows"), lax.axis_index("grp")
    z, y, c = rows_at // (2 * NY), (rows_at // 2) % NY, rows_at % 2
    rows = slab.shape[0]
    step = rows // LOADS

    def send(src, dst, at, recv, peer):
        pltpu.make_async_remote_copy(
            src_ref=src, dst_ref=dst, send_sem=send_sem.at[at], recv_sem=recv,
            device_id=place(*peer), device_id_type=MESH,
        ).start()

    def hops(dy, dx):
        return min(dy, NY - dy) + min(dx, NX - dx)

    chips = sorted(((dy, dx) for dy in range(NY) for dx in range(NX)), key=lambda d: -hops(*d))

    sketch_copy = pltpu.make_async_copy(sketch, sketch_v, load_sem.at[LOADS])
    sketch_copy.start()
    loads = [
        pltpu.make_async_copy(slab.at[pl.ds(i * step, step)], slab_v.at[pl.ds(i * step, step)], load_sem.at[i])
        for i in range(LOADS)
    ]
    for load in loads:
        load.start()

    barrier = pltpu.get_barrier_semaphore()
    peers = [((z + d) % NZ, y, c, x) for d in (4, 12, 3, 13, 2, 14, 1, 15)] + [
        (z, (y + dy) % NY, (c + dc) % 2, (x + dx) % NX)
        for dy, dx in chips for dc in range(2) if (dy, dx, dc) != (0, 0, 0)
    ]
    for peer in peers:
        pl.semaphore_signal(barrier, inc=1, device_id=place(*peer), device_id_type=MESH)

    sketch_copy.wait()
    for i, load in enumerate(loads):
        load.wait()
        first[pl.ds(i * step, step), :] = jnp.dot(
            slab_v[pl.ds(i * step, step), :], sketch_v[...], preferred_element_type=F32
        )

    whole = first[...]
    whole_t = whole.T
    local = jnp.dot(whole_t, whole, precision=lax.Precision.HIGHEST, preferred_element_type=F32)
    for q in range(16):
        gram0[q] = local[8 * q : 8 * q + 8, :]
    high = whole_t.astype(BF16)
    low = (whole_t - high.astype(F32)).astype(BF16)
    first_t[...] = jnp.concatenate([high, low], 0)

    def product(j):
        both = jnp.dot(first_t[...], slab_v[:, j * 512 : (j + 1) * 512], preferred_element_type=F32)
        sums = both[:128] + both[128:]
        for k in range(4):
            block = sums[:, k * 128 : (k + 1) * 128].T
            for yl in range(2):
                for cc in range(2):
                    for xx in range(4):
                        row = ((yl * 2 + cc) * 4 + xx) * 8
                        yy = 2 * (k % 2) + yl
                        a, b = (xx, yy) if j % 2 == 0 else (yy, xx)
                        part[cc, j, a, b, k // 2] = block[row : row + 8, :]

    def peer_of(j, phase, d):
        if (j + phase) % 2 == 0:
            return (z, y, c, (x + d) % NX)
        return (z, (y + d) % NY, c, x)

    def index_of(j, phase, d):
        return (x + d) % NX if (j + phase) % 2 == 0 else (y + d) % NY

    def to_core(j):
        send(part.at[1 - c, j], got0.at[j], 1, recv0.at[j], (z, y, 1 - c, x))

    def to_first_axis(j):
        wait_bytes(got0.at[j], recv0.at[j])
        for d in (2, 1, 3, 0):
            a = index_of(j, 0, d)
            part[c, j, a] = part[c, j, a] + got0[j, a]
            if d:
                send(part.at[c, j, a], got1.at[j, d - 1], 2, recv1.at[j], peer_of(j, 0, d))

    def to_second_axis(j):
        wait_bytes(got1.at[j], recv1.at[j])
        a = index_of(j, 0, 0)
        for d in (2, 1, 3, 0):
            b = index_of(j, 1, d)
            sum1[j, b] = (part[c, j, a, b] + got1[j, 0, b]) + (got1[j, 1, b] + got1[j, 2, b])
            if d:
                send(sum1.at[j, b], got2.at[j, d - 1], 4, recv2.at[j], peer_of(j, 1, d))

    def to_planes(j):
        wait_bytes(got2.at[j], recv2.at[j])
        b = index_of(j, 1, 0)
        sum2[pl.ds(2 * j, 2)] = (sum1[j, b] + got2[j, 0]) + (got2[j, 1] + got2[j, 2])
        for to in range(2 * j, 2 * j + 2):
            @pl.when(z != to)
            def _():
                send(sum2.at[to], got3.at[z], 5, recv3.at[0], (to, y, c, x))


    pl.semaphore_wait(barrier, len(peers))
    for d in (4, 12):
        pl.semaphore_signal(ready, inc=1, device_id=place((z + d) % NZ, y, c, x), device_id_type=MESH)

    at_y, at_x = (y + 1) % NY, (x + 1) % NX
    is_owner = (at_y < 3) & (at_x < 3) & (at_y + at_x > 0)
    own = 2 * (3 * at_y + at_x - 1) + c
    slot = (y * NX + x) * 2 + c

    def unless_here(to_y, to_c, to_x):
        return pl.when((y != to_y) | (x != to_x) | (c != to_c))

    for q in (14, 15, 12, 13, 8, 9, 2, 3, 10, 11, 6, 7, 4, 5, 0, 1):
        to = owner_of(q)

        @unless_here(*to)
        def _():
            send(gram0.at[q], gotg1.at[slot], 0, recvg.at[0], (z, *to))

    @pl.when(is_owner)
    def _():
        gotg1[slot] = gram0[own]

    for j in range(8):
        product(j)
        to_core(j)
        if j >= 4:
            to_first_axis(j - 4)

    for j in range(4, 4):
        to_first_axis(j)

    pl.semaphore_wait(ready, 2)

    @pl.when(is_owner)
    def _():
        wait_bytes(gotg1.at[pl.ds(0, 31)], recvg.at[0])
        tile = gotg1[0]
        for s in range(1, 32):
            tile = tile + gotg1[s]
        gotg2[z] = tile
        for to in range(NZ):
            @pl.when(z != to)
            def _():
                send(gotg2.at[z], gotg2.at[z], 3, recvg.at[1], (to, y, c, x))

    for j in range(4, 8):
        to_first_axis(j)

    for j in range(8):
        to_second_axis(j)
    for j in range(4):
        to_planes(j)

    @pl.when(is_owner)
    def _():
        wait_bytes(gotg2.at[pl.ds(0, 15)], recvg.at[1])
        tile = gotg2[0]
        for s in range(1, NZ):
            tile = tile + gotg2[s]
        gram[own] = tile
        for to_y, to_x in sorted(((v, u) for v in range(NY) for u in range(NX)), key=sum):
            for to_c in (1, 0):
                @unless_here(to_y, to_c, to_x)
                def _():
                    send(gram.at[own], gram.at[own], 6, recvg.at[2], (z, to_y, to_c, to_x))

    for j in range(4, 8):
        to_planes(j)

    @pl.when(is_owner)
    def _():
        wait_bytes(gram.at[pl.ds(0, 15)], recvg.at[2])

    @pl.when(jnp.logical_not(is_owner))
    def _():
        wait_bytes(gram, recvg.at[2])

    for i, tile in enumerate(inverse_factor([gram[q] for q in range(16)])):
        inverse[8 * i : 8 * i + 8, :] = tile

    got3[z] = sum2[z]
    wait_bytes(got3.at[pl.ds(0, 15)], recv3.at[0])
    total = got3[0]
    for s in range(1, NZ):
        total = total + got3[s]
    final[...] = total

    @pl.when(is_owner)
    def _():
        wait_bytes(gram0.at[pl.ds(0, 15)], send_sem.at[0])
        wait_bytes(gotg2.at[pl.ds(0, 15)], send_sem.at[3])
        wait_bytes(gotg1.at[pl.ds(0, 31)], send_sem.at[6])

    @pl.when(jnp.logical_not(is_owner))
    def _():
        wait_bytes(gram0, send_sem.at[0])

    wait_bytes(got0, send_sem.at[1])
    wait_bytes(got1, send_sem.at[2])
    wait_bytes(got2, send_sem.at[4])
    wait_bytes(got3.at[pl.ds(0, 15)], send_sem.at[5])


def local(slab, sketch):
    rows, width = slab.shape
    rank = sketch.shape[1]
    total_rows = rows * lax.axis_size(("rows", "grp"))
    vmem = pl.BlockSpec(memory_space=pltpu.VMEM)
    tiles = lambda *lead: pltpu.VMEM((*lead, 8, 128), F32)
    first, inverse, final = pl.pallas_call(
        exchange,
        out_shape=[pltpu.VMEM((rows, rank), F32), pltpu.VMEM((rank, rank), F32), pltpu.VMEM((8, 128), F32)],
        in_specs=[pl.BlockSpec(memory_space=pl.ANY)] * 2,
        out_specs=[vmem] * 3,
        scratch_shapes=[
            pltpu.VMEM((rows, width), BF16),
            pltpu.VMEM((width, rank), BF16),
            pltpu.VMEM((2 * rank, rows), BF16),
            tiles(2, 8, 4, 4, 2),
            tiles(8, 4, 4, 2),
            tiles(8, 3, 4, 2),
            tiles(8, 4, 2),
            tiles(8, 3, 2),
            tiles(16),
            tiles(16),
            tiles(16),
            tiles(32),
            tiles(16),
            tiles(16),
            pltpu.SemaphoreType.DMA((LOADS + 1,)),
            pltpu.SemaphoreType.DMA((7,)),
            pltpu.SemaphoreType.DMA((8,)),
            pltpu.SemaphoreType.DMA((8,)),
            pltpu.SemaphoreType.DMA((8,)),
            pltpu.SemaphoreType.DMA((1,)),
            pltpu.SemaphoreType.DMA((3,)),
            pltpu.SemaphoreType.REGULAR,
        ],
        compiler_params=pltpu.CompilerParams(
            collective_id=0, has_side_effects=True, vmem_limit_bytes=24 * 2**20
        ),
    )(*(pltpu.with_memory_space_constraint(array, pltpu.HBM) for array in (slab, sketch)))
    basis, projected = pl.pallas_call(
        functools.partial(finish, math.sqrt(total_rows), math.sqrt(width / total_rows)),
        out_shape=[jax.ShapeDtypeStruct((rows, rank), F32), jax.ShapeDtypeStruct((8, 128), BF16)],
        compiler_params=pltpu.CompilerParams(vmem_limit_bytes=8 * 2**20),
    )(*(pltpu.with_memory_space_constraint(array, pltpu.VMEM) for array in (first, inverse, final)))
    return (basis, projected)


def solution(mesh):
    return jax.shard_map(
        local,
        mesh=mesh,
        in_specs=(P(("rows", "grp"), None), P()),
        out_specs=(P(("rows", "grp"), None), P(("rows", "grp"), None)),
        check_vma=False,
    )
```

```python
import functools
import math

import jax
import jax.numpy as jnp
from jax import lax
from jax.experimental import pallas as pl
from jax.experimental.pallas import tpu as pltpu
from jax.sharding import PartitionSpec as P

MESH = pl.DeviceIdType.MESH
F32, BF16 = jnp.float32, jnp.bfloat16
NZ, NY, NX = 16, 4, 4
LOADS = 4


def place(z, y, c, x):
    return {"rows": (z * NY + y) * 2 + c, "grp": x}


def wait_bytes(ref, sem):
    pltpu.make_async_copy(ref, ref, sem).wait()


def lanes(tile, at):
    return jnp.broadcast_to(tile[:, at : at + 1], tile.shape)


def sublanes(tile, at):
    return jnp.broadcast_to(tile[at : at + 1, :], tile.shape)


def inverse_factor(gram):
    blocks = len(gram)
    shape = gram[0].shape
    row = lax.broadcasted_iota(jnp.int32, shape, 0)
    column = lax.broadcasted_iota(jnp.int32, shape, 1)
    left = list(gram)
    out = []
    for b in range(blocks):
        tile = left[b]
        cols = [lanes(tile, 8 * b + j) for j in range(8)]
        here = (column >= 8 * b) & (column < 8 * b + 8)
        tile = jnp.where(here, jnp.where(column == row + 8 * b, 1.0, 0.0), tile)
        own = {(i, l): sublanes(cols[l], i) for i in range(8) for l in range(i, 8)}
        over, factor = {}, {}
        for j in range(8):
            over[j] = 1.0 / own[j, j]
            for i in range(j + 1, 8):
                factor[i, j] = own[j, i] * over[j]
            for i in range(j + 1, 8):
                for l in range(i, 8):
                    own[i, l] = own[i, l] - factor[i, j] * own[j, l]
        rows = [sublanes(tile, j) for j in range(8)]
        for j in range(8):
            for i in range(j + 1, 8):
                rows[i] = rows[i] - factor[i, j] * rows[j]
        pivots, done = own[0, 0], rows[0]
        for j in range(1, 8):
            pivots = jnp.where(row == j, own[j, j], pivots)
            done = jnp.where(row == j, rows[j], done)
        out.append(jnp.where(column < 8 * b + 8, done * lax.rsqrt(pivots), 0.0))
        for i in range(b + 1, blocks):
            cols = [lanes(left[i], 8 * b + j) for j in range(8)]
            rest = jnp.where(here, 0.0, left[i])
            for j in range(8):
                times = cols[j] * over[j]
                for l in range(j + 1, 8):
                    cols[l] = cols[l] - times * own[j, l]
                rest = rest - times * rows[j]
            left[i] = rest
    return out


def thirds(matrix):
    high = matrix.astype(BF16)
    rest = matrix - high.astype(F32)
    middle = rest.astype(BF16)
    return high, middle, (rest - middle.astype(F32)).astype(BF16)


def finish(basis_scale, projected_scale, first, inverse, final, basis, projected):
    high, middle, low = thirds(inverse[...])
    right = jnp.concatenate([high, high, middle, high, middle, low], 1)

    def apply(matrix):
        h, m, l = thirds(matrix)
        return lax.dot_general(
            jnp.concatenate([h, m, h, l, m, h], 1), right, (((1,), (1,)), ((), ())), preferred_element_type=F32
        )

    basis[...] = apply(first[...]) * basis_scale
    projected[...] = (apply(final[...]) * projected_scale).astype(BF16)


def owner_of(tile):
    at = tile // 2 + 1
    return (at // 3 + 3) % NY, tile % 2, (at % 3 + 3) % NX


def exchange(
    slab, sketch, first, inverse, final,
    slab_v, sketch_v, first_t, part, got0, got1, sum1, got2, sum2, got3,
    gram0, gotg1, gotg2, gram,
    load_sem, send_sem, recv0, recv1, recv2, recv3, recvg, ready,
):
    rows_at, x = lax.axis_index("rows"), lax.axis_index("grp")
    z, y, c = rows_at // (2 * NY), (rows_at // 2) % NY, rows_at % 2
    rows = slab.shape[0]
    step = rows // LOADS

    def send(src, dst, at, recv, peer):
        pltpu.make_async_remote_copy(
            src_ref=src, dst_ref=dst, send_sem=send_sem.at[at], recv_sem=recv,
            device_id=place(*peer), device_id_type=MESH,
        ).start()

    def hops(dy, dx):
        return min(dy, NY - dy) + min(dx, NX - dx)

    chips = sorted(((dy, dx) for dy in range(NY) for dx in range(NX)), key=lambda d: -hops(*d))

    sketch_copy = pltpu.make_async_copy(sketch, sketch_v, load_sem.at[LOADS])
    sketch_copy.start()
    loads = [
        pltpu.make_async_copy(slab.at[pl.ds(i * step, step)], slab_v.at[pl.ds(i * step, step)], load_sem.at[i])
        for i in range(LOADS)
    ]
    for load in loads:
        load.start()

    barrier = pltpu.get_barrier_semaphore()
    peers = [((z + d) % NZ, y, c, x) for d in (4, 12, 3, 13, 2, 14, 1, 15)] + [
        (z, (y + dy) % NY, (c + dc) % 2, (x + dx) % NX)
        for dy, dx in chips for dc in range(2) if (dy, dx, dc) != (0, 0, 0)
    ]
    for peer in peers:
        pl.semaphore_signal(barrier, inc=1, device_id=place(*peer), device_id_type=MESH)

    sketch_copy.wait()
    for i, load in enumerate(loads):
        load.wait()
        first[pl.ds(i * step, step), :] = jnp.dot(
            slab_v[pl.ds(i * step, step), :], sketch_v[...], preferred_element_type=F32
        )

    whole = first[...]
    whole_t = whole.T
    local = jnp.dot(whole_t, whole, precision=lax.Precision.HIGHEST, preferred_element_type=F32)
    for q in range(16):
        gram0[q] = local[8 * q : 8 * q + 8, :]
    high = whole_t.astype(BF16)
    low = (whole_t - high.astype(F32)).astype(BF16)
    first_t[...] = jnp.concatenate([high, low], 0)

    def product(j):
        both = jnp.dot(first_t[...], slab_v[:, j * 512 : (j + 1) * 512], preferred_element_type=F32)
        sums = both[:128] + both[128:]
        for k in range(4):
            block = sums[:, k * 128 : (k + 1) * 128].T
            for yl in range(2):
                for cc in range(2):
                    for xx in range(4):
                        row = ((yl * 2 + cc) * 4 + xx) * 8
                        yy = 2 * (k % 2) + yl
                        a, b = (xx, yy) if j % 2 == 0 else (yy, xx)
                        part[cc, j, a, b, k // 2] = block[row : row + 8, :]

    def peer_of(j, phase, d):
        if (j + phase) % 2 == 0:
            return (z, y, c, (x + d) % NX)
        return (z, (y + d) % NY, c, x)

    def index_of(j, phase, d):
        return (x + d) % NX if (j + phase) % 2 == 0 else (y + d) % NY

    def to_core(j):
        send(part.at[1 - c, j], got0.at[j], 1, recv0.at[j], (z, y, 1 - c, x))

    def to_first_axis(j):
        wait_bytes(got0.at[j], recv0.at[j])
        for d in (2, 1, 3, 0):
            a = index_of(j, 0, d)
            part[c, j, a] = part[c, j, a] + got0[j, a]
            if d:
                send(part.at[c, j, a], got1.at[j, d - 1], 2, recv1.at[j], peer_of(j, 0, d))

    def to_second_axis(j):
        wait_bytes(got1.at[j], recv1.at[j])
        a = index_of(j, 0, 0)
        for d in (2, 1, 3, 0):
            b = index_of(j, 1, d)
            sum1[j, b] = (part[c, j, a, b] + got1[j, 0, b]) + (got1[j, 1, b] + got1[j, 2, b])
            if d:
                send(sum1.at[j, b], got2.at[j, d - 1], 4, recv2.at[j], peer_of(j, 1, d))

    def to_planes(j):
        wait_bytes(got2.at[j], recv2.at[j])
        b = index_of(j, 1, 0)
        sum2[pl.ds(2 * j, 2)] = (sum1[j, b] + got2[j, 0]) + (got2[j, 1] + got2[j, 2])
        for to in range(2 * j, 2 * j + 2):
            @pl.when(z != to)
            def _():
                send(sum2.at[to], got3.at[z], 5, recv3.at[0], (to, y, c, x))


    pl.semaphore_wait(barrier, len(peers))
    for d in (4, 12):
        pl.semaphore_signal(ready, inc=1, device_id=place((z + d) % NZ, y, c, x), device_id_type=MESH)

    at_y, at_x = (y + 1) % NY, (x + 1) % NX
    is_owner = (at_y < 3) & (at_x < 3) & (at_y + at_x > 0)
    own = 2 * (3 * at_y + at_x - 1) + c
    slot = (y * NX + x) * 2 + c

    def unless_here(to_y, to_c, to_x):
        return pl.when((y != to_y) | (x != to_x) | (c != to_c))

    for q in (14, 15, 12, 13, 8, 9, 2, 3, 10, 11, 6, 7, 4, 5, 0, 1):
        to = owner_of(q)

        @unless_here(*to)
        def _():
            send(gram0.at[q], gotg1.at[slot], 0, recvg.at[0], (z, *to))

    @pl.when(is_owner)
    def _():
        gotg1[slot] = gram0[own]

    for j in range(8):
        product(j)
        to_core(j)
        if j >= 4:
            to_first_axis(j - 4)

    for j in range(4, 4):
        to_first_axis(j)

    pl.semaphore_wait(ready, 2)

    @pl.when(is_owner)
    def _():
        wait_bytes(gotg1.at[pl.ds(0, 31)], recvg.at[0])
        tile = gotg1[0]
        for s in range(1, 32):
            tile = tile + gotg1[s]
        gotg2[z] = tile
        for to in range(NZ):
            @pl.when(z != to)
            def _():
                send(gotg2.at[z], gotg2.at[z], 3, recvg.at[1], (to, y, c, x))

    for j in range(4, 8):
        to_first_axis(j)

    for j in range(8):
        to_second_axis(j)
    for j in range(4):
        to_planes(j)

    @pl.when(is_owner)
    def _():
        wait_bytes(gotg2.at[pl.ds(0, 15)], recvg.at[1])
        tile = gotg2[0]
        for s in range(1, NZ):
            tile = tile + gotg2[s]
        gram[own] = tile
        for to_y, to_x in sorted(((v, u) for v in range(NY) for u in range(NX)), key=sum):
            for to_c in (1, 0):
                @unless_here(to_y, to_c, to_x)
                def _():
                    send(gram.at[own], gram.at[own], 6, recvg.at[2], (z, to_y, to_c, to_x))

    for j in range(4, 8):
        to_planes(j)

    @pl.when(is_owner)
    def _():
        wait_bytes(gram.at[pl.ds(0, 15)], recvg.at[2])

    @pl.when(jnp.logical_not(is_owner))
    def _():
        wait_bytes(gram, recvg.at[2])

    for i, tile in enumerate(inverse_factor([gram[q] for q in range(16)])):
        inverse[8 * i : 8 * i + 8, :] = tile

    got3[z] = sum2[z]
    wait_bytes(got3.at[pl.ds(0, 15)], recv3.at[0])
    total = got3[0]
    for s in range(1, NZ):
        total = total + got3[s]
    final[...] = total

    @pl.when(is_owner)
    def _():
        wait_bytes(gram0.at[pl.ds(0, 15)], send_sem.at[0])
        wait_bytes(gotg2.at[pl.ds(0, 15)], send_sem.at[3])
        wait_bytes(gotg1.at[pl.ds(0, 31)], send_sem.at[6])

    @pl.when(jnp.logical_not(is_owner))
    def _():
        wait_bytes(gram0, send_sem.at[0])

    wait_bytes(got0, send_sem.at[1])
    wait_bytes(got1, send_sem.at[2])
    wait_bytes(got2, send_sem.at[4])
    wait_bytes(got3.at[pl.ds(0, 15)], send_sem.at[5])


def local(slab, sketch):
    rows, width = slab.shape
    rank = sketch.shape[1]
    total_rows = rows * lax.axis_size(("rows", "grp"))
    vmem = pl.BlockSpec(memory_space=pltpu.VMEM)
    tiles = lambda *lead: pltpu.VMEM((*lead, 8, 128), F32)
    first, inverse, final = pl.pallas_call(
        exchange,
        out_shape=[pltpu.VMEM((rows, rank), F32), pltpu.VMEM((rank, rank), F32), pltpu.VMEM((8, 128), F32)],
        in_specs=[pl.BlockSpec(memory_space=pl.ANY)] * 2,
        out_specs=[vmem] * 3,
        scratch_shapes=[
            pltpu.VMEM((rows, width), BF16),
            pltpu.VMEM((width, rank), BF16),
            pltpu.VMEM((2 * rank, rows), BF16),
            tiles(2, 8, 4, 4, 2),
            tiles(8, 4, 4, 2),
            tiles(8, 3, 4, 2),
            tiles(8, 4, 2),
            tiles(8, 3, 2),
            tiles(16),
            tiles(16),
            tiles(16),
            tiles(32),
            tiles(16),
            tiles(16),
            pltpu.SemaphoreType.DMA((LOADS + 1,)),
            pltpu.SemaphoreType.DMA((7,)),
            pltpu.SemaphoreType.DMA((8,)),
            pltpu.SemaphoreType.DMA((8,)),
            pltpu.SemaphoreType.DMA((8,)),
            pltpu.SemaphoreType.DMA((1,)),
            pltpu.SemaphoreType.DMA((3,)),
            pltpu.SemaphoreType.REGULAR,
        ],
        compiler_params=pltpu.CompilerParams(
            collective_id=0, has_side_effects=True, vmem_limit_bytes=24 * 2**20
        ),
    )(*(pltpu.with_memory_space_constraint(array, pltpu.HBM) for array in (slab, sketch)))
    basis, projected = pl.pallas_call(
        functools.partial(finish, math.sqrt(total_rows), math.sqrt(width / total_rows)),
        out_shape=[jax.ShapeDtypeStruct((rows, rank), F32), jax.ShapeDtypeStruct((8, 128), BF16)],
        compiler_params=pltpu.CompilerParams(vmem_limit_bytes=8 * 2**20),
    )(*(pltpu.with_memory_space_constraint(array, pltpu.VMEM) for array in (first, inverse, final)))
    return (basis, projected)


def solution(mesh):
    return jax.shard_map(
        local,
        mesh=mesh,
        in_specs=(P(("rows", "grp"), None), P()),
        out_specs=(P(("rows", "grp"), None), P(("rows", "grp"), None)),
        check_vma=False,
    )
```
